32 devices in a mesh: face: 2 (over core), elem: 16 (over z, y, x).
Axes of the slice: x: 2, y: 2, z: 4, core: 2. Of those that a mesh axis runs over, the one named last changes fastest.
Arguments:
- state: float32 [432, 32, 2048], P(None, 'face', 'elem'), may hold values from -6 to 6
- speed_x: float32 [432], replicated, may hold values from -0.25 to 0.25
- speed_y: float32 [432], replicated, may hold values from -0.25 to 0.25
- w_in: bfloat16 [512, 432], replicated, may hold values from -0.3125 to 0.3125
- b_in: float32 [512], replicated, may hold values from -1.8 to 1.8
- w_mid: bfloat16 [512, 512], replicated, may hold values from -0.25 to 0.25
- b_mid: float32 [512], replicated, may hold values from -1.8 to 1.8
- w_top: bfloat16 [512, 512], replicated, may hold values from -0.25 to 0.25
- b_top: float32 [512], replicated, may hold values from -1.8 to 1.8
- w_out: bfloat16 [360, 512], replicated, may hold values from -0.25 to 0.25
- b_out: float32 [360], replicated, may hold values from -1.8 to 1.8
- span_of: int32 [2, 16, 2048, 1], P('face', 'elem'), may hold values from 0 to 31; in each aligned block of 2048 rows (0 to 2047, 2048 to 4095, ..., all dimensions but the last counted through in order) at most 128 rows name the same one
Outputs:
- final_state: float32 [432, 32, 2048], P(None, 'face', 'elem')
- tendencies: bfloat16 [360, 32, 2048], P(None, 'face', 'elem')
- span_heating: float32 [32], P(('face', 'elem'))
The draws below stay inside these ranges and needn't reach their ends.
Inputs may be any that keep to these rules, and one draw needn't show every extreme that they name: `span_of`: among the columns of one device, no span is named more than 128 times, a bound that some block reaches; every span is named by some column.
All inputs are finite; a program needn't handle non-finite values.
Results may differ from the reference program's by a relative error of at most 0.0095.
Values may be sent and summed in bfloat16 or wider, within the bound.
A program may use at most 128 MiB of HBM per device.

```python
import math
import jax
import jax.numpy as jnp
import numpy as np
from jax import lax

NP = 4
LEV = 72
HID = 512
F_IN = 432
F_OUT = 360
PX = 128
PY = 16
NPX = 2048
NPY = 32
COLS_DEV = 2048
CAP = 128
N_FACE = 2
N_ELEM = 16
DEVICES = 32


def block_levels(rng, shape, cuts, low, high):
    def one(axis_at, blocks):
        steps = jax.random.uniform(jax.random.fold_in(jax.random.fold_in(rng, 6), axis_at), (blocks,), jnp.float32, low / len(cuts), high / len(cuts))
        return jnp.repeat(jnp.exp(steps), shape[axis_at] // blocks).reshape((-1,) + (1,) * (len(shape) - axis_at - 1))

    level = one(*cuts[0])
    for cut in cuts[1:]:
        level = level * one(*cut)
    return level


def deal_out(own_key, own, number, rows, amount, top, reach, lean):
    ranking = jax.random.permutation(own_key, amount)
    packed, usual = shares(amount, rows * top, reach, lean, True), shares(amount, rows * top, reach, lean, False)
    places = jnp.arange(amount)

    def named(lengths, turn):
        used = int((lengths > 0).sum())
        fixed = max(1, used // 4)
        moved = fixed + (places - fixed + turn * (used - fixed)) % max(1, amount - fixed)
        return jnp.zeros((amount,), jnp.int32).at[ranking[jnp.where(places < fixed, places, moved)]].set(jnp.asarray(lengths, jnp.int32))

    lengths = jnp.where(number % 4 == 0, named(packed, number // 4), named(usual, number - number // 4 - 1))
    mixed = jax.random.permutation(jax.random.fold_in(own, 3), amount)
    giver, sink = mixed[0:amount // 2 * 2:2], mixed[1:amount // 2 * 2:2]
    slack = jnp.minimum(lengths[giver] - 1, reach - lengths[sink]) // 2
    slack = jnp.where((giver == ranking[0]) | (sink == ranking[0]) | (lengths[sink] == 0), 0, jnp.maximum(slack, 0))
    moved = jax.random.randint(jax.random.fold_in(own, 4), (amount // 2,), 0, 1 << 20) % (slack + 1)
    lengths = lengths.at[giver].add(-moved).at[sink].add(moved)
    items = jnp.searchsorted(jnp.cumsum(lengths), jnp.arange(rows * top), side="right").astype(jnp.int32)
    table = items.reshape(top, rows).T
    table = table[jax.random.permutation(jax.random.fold_in(own, 1), rows)]
    turn = jax.random.randint(jax.random.fold_in(own, 2), (rows, 1), 0, top)
    return jnp.take_along_axis(table, (jnp.arange(top)[None, :] + turn) % top, axis=1)


def shares(amount, total, limit, lean, full):
    portions = [(1 << 20) // math.isqrt(grade ** lean) + 1 for grade in range(1, amount + 1)]
    largest = limit if full else min(limit, max(-(-total // amount), total * portions[0] // sum(portions)))
    least = 1 if total - largest >= amount - 1 else 0
    holding, rest = [largest] + [least] * (amount - 1), total - largest - least * (amount - 1)
    while rest > 0:
        free = [i for i in range(1, amount) if holding[i] < largest] or [i for i in range(1, amount) if holding[i] < limit]
        mass, budget = sum([portions[i] for i in free]), rest
        for i in free:
            extra = min(limit - holding[i], max(1, budget * portions[i] // mass), rest)
            holding[i] = holding[i] + extra
            rest = rest - extra
    return np.array(holding)


def gaussian(own_key, shape, deviation, most, shards=(), dtype=jnp.bfloat16):
    factor_of = block_levels(own_key, shape, shards, -0.22, 0.18) if shards else 1.0
    entries = jax.random.normal(own_key, shape, jnp.float32) * deviation * factor_of
    return jnp.minimum(jnp.maximum(entries, -most), most).astype(dtype)


def setup_inputs(seed: int = 0) -> dict:
    key_list = jax.random.split(jax.random.key(seed), 13)
    state = gaussian(key_list[0], (F_IN, NPY, NPX), 1.0, 6.0, ((1, 2), (2, 16)), jnp.float32)
    speed_x = jnp.clip(jax.random.uniform(key_list[1], (F_IN,), jnp.float32, -0.25, 0.25), -0.25, 0.25)
    speed_y = jnp.clip(jax.random.uniform(key_list[2], (F_IN,), jnp.float32, -0.25, 0.25), -0.25, 0.25)
    w_in = gaussian(key_list[3], (HID, F_IN), F_IN ** -0.5, 0.3125)
    b_in = gaussian(key_list[4], (HID,), 0.3, 1.8, (), jnp.float32)
    w_mid = gaussian(key_list[5], (HID, HID), HID ** -0.5, 0.25)
    b_mid = gaussian(key_list[6], (HID,), 0.3, 1.8, (), jnp.float32)
    w_top = gaussian(key_list[7], (HID, HID), HID ** -0.5, 0.25)
    b_top = gaussian(key_list[8], (HID,), 0.3, 1.8, (), jnp.float32)
    w_out = gaussian(key_list[9], (F_OUT, HID), HID ** -0.5, 0.25)
    b_out = gaussian(key_list[10], (F_OUT,), 0.3, 1.8, (), jnp.float32)
    span_of_keys = jax.random.split(jax.random.fold_in(key_list[11], 1), N_FACE * N_ELEM * COLS_DEV // COLS_DEV)
    span_of_turns = jax.random.permutation(jax.random.fold_in(key_list[11], 3), N_FACE * N_ELEM * COLS_DEV // COLS_DEV)
    span_of = jax.vmap(lambda own, number: deal_out(jax.random.fold_in(key_list[11], 2), own, number, COLS_DEV, DEVICES, 1, CAP, 2))(span_of_keys, span_of_turns).reshape((N_FACE, N_ELEM, COLS_DEV, 1))
    return {"state": state, "speed_x": speed_x, "speed_y": speed_y, "w_in": w_in, "b_in": b_in, "w_mid": w_mid, "b_mid": b_mid, "w_top": w_top, "b_top": b_top, "w_out": w_out, "b_out": b_out, "span_of": span_of}


def gll_matrix():
    inner_node = 1.0 / math.sqrt(5.0)
    gll_nodes = np.array([-1.0, -inner_node, inner_node, 1.0])
    weights = np.array([1.0 / np.prod([gll_nodes[outer] - gll_nodes[other] for other in range(4) if other != outer]) for outer in range(4)])
    matrix = np.zeros((4, 4))
    for outer in range(4):
        for inner in range(4):
            if inner != outer:
                matrix[outer, inner] = weights[inner] / weights[outer] / (gll_nodes[outer] - gll_nodes[inner])
    for outer in range(4):
        matrix[outer, outer] = -np.sum(matrix[outer])
    return matrix.astype(np.float32)

def stiff_x(tendency):
    feats, height, breadth = tendency.shape
    blocks = tendency.reshape(feats, height, breadth // NP, NP)
    first_pts = blocks[..., 0]
    last_pts = blocks[..., NP - 1]
    new_last = 0.5 * (last_pts + jnp.roll(first_pts, -1, axis=2))
    new_first = jnp.roll(new_last, 1, axis=2)
    blocks = blocks.at[..., 0].set(new_first).at[..., NP - 1].set(new_last)
    return blocks.reshape(tendency.shape)

def stiff_y(tendency):
    feats, height, breadth = tendency.shape
    blocks = tendency.reshape(feats, height // NP, NP, breadth)
    first_pts = blocks[:, :, 0, :]
    last_pts = blocks[:, :, NP - 1, :]
    new_last = 0.5 * (last_pts + jnp.roll(first_pts, -1, axis=1))
    new_first = jnp.roll(new_last, 1, axis=1)
    blocks = blocks.at[:, :, 0, :].set(new_first).at[:, :, NP - 1, :].set(new_last)
    return blocks.reshape(tendency.shape)

def operator(field, speed_x, speed_y):
    deriv_table = jnp.asarray(gll_matrix())
    feats, height, breadth = field.shape
    along_x = jnp.einsum('ji,fyei->fyej', deriv_table, field.reshape(feats, height, breadth // NP, NP), precision=lax.Precision.HIGHEST).reshape(field.shape)
    along_y = jnp.einsum('ji,feix->fejx', deriv_table, field.reshape(feats, height // NP, NP, breadth), precision=lax.Precision.HIGHEST).reshape(field.shape)
    tendency = -(speed_x[:, None, None] * along_x + speed_y[:, None, None] * along_y)
    return stiff_y(stiff_x(tendency))

def advance(pieces):
    field, speed_x, speed_y = pieces
    section_one = field + operator(field, speed_x, speed_y)
    section_two = 0.75 * field + 0.25 * (section_one + operator(section_one, speed_x, speed_y))
    return field / 3.0 + 2.0 / 3.0 * (section_two + operator(section_two, speed_x, speed_y))

def column_model(inputs, w_in, b_in, w_mid, b_mid, w_top, b_top, w_out, b_out):
    hidden = jax.nn.silu(jnp.dot(w_in, inputs, preferred_element_type=jnp.float32) + b_in[:, None]).astype(jnp.bfloat16)
    hidden = jax.nn.silu(jnp.dot(w_mid, hidden, preferred_element_type=jnp.float32) + b_mid[:, None]).astype(jnp.bfloat16)
    hidden = jax.nn.silu(jnp.dot(w_top, hidden, preferred_element_type=jnp.float32) + b_top[:, None]).astype(jnp.bfloat16)
    outputs = jnp.dot(w_out, hidden, preferred_element_type=jnp.float32) + b_out[:, None]
    heating = lax.optimization_barrier(jnp.sum(outputs[:LEV], axis=0))
    return (outputs.astype(jnp.bfloat16), heating)

def reference(state, speed_x, speed_y, w_in, b_in, w_mid, b_mid, w_top, b_top, w_out, b_out, span_of):
    feature_block = math.gcd(F_IN, 48)
    groups = F_IN // feature_block
    final_state = lax.map(advance, (state.reshape(groups, feature_block, NPY, NPX), speed_x.reshape(groups, feature_block), speed_y.reshape(groups, feature_block)))
    final_state = final_state.reshape(F_IN, NPY, NPX)
    columns = final_state.reshape(F_IN, N_FACE, PY, N_ELEM, PX).transpose(1, 3, 0, 2, 4).reshape(DEVICES, F_IN, COLS_DEV).astype(jnp.bfloat16)

    def physics(inputs):
        return column_model(inputs, w_in, b_in, w_mid, b_mid, w_top, b_top, w_out, b_out)
    tend_cols, heating = lax.map(physics, columns)
    target = span_of.reshape(DEVICES * COLS_DEV).astype(jnp.int32)
    span_heating = jax.ops.segment_sum(heating.reshape(DEVICES * COLS_DEV), target, DEVICES) / COLS_DEV
    tendencies = tend_cols.reshape(N_FACE, N_ELEM, F_OUT, PY, PX).transpose(2, 0, 3, 1, 4).reshape(F_OUT, NPY, NPX)
    return (final_state, tendencies, span_heating)
```

```python
import functools
import math

import jax
import jax.numpy as jnp
import numpy as np
from jax import lax
from jax.experimental import pallas as pl
from jax.experimental.pallas import tpu as pltpu
from jax.sharding import PartitionSpec as P

NP = 4
LEV = 72
CHUNKS = 3
MESH = pl.DeviceIdType.MESH
SX_SLOT = (0, 1, 6, 7)
SY_SLOT = (2, 3, 4, 5)


def gll_matrix():
    inner_node = 1.0 / math.sqrt(5.0)
    nodes = np.array([-1.0, -inner_node, inner_node, 1.0])
    weights = np.array(
        [1.0 / np.prod([nodes[j] - nodes[k] for k in range(4) if k != j]) for j in range(4)]
    )
    matrix = np.zeros((4, 4))
    for i in range(4):
        for j in range(4):
            if i != j:
                matrix[i, j] = weights[j] / weights[i] / (nodes[i] - nodes[j])
    for i in range(4):
        matrix[i, i] = -np.sum(matrix[i])
    return matrix


def operator_tables(breadth):
    table = gll_matrix()
    deriv = np.kron(np.eye(breadth // NP), table)
    avg = np.eye(breadth)
    for j in range(breadth):
        if j % NP == NP - 1:
            avg[j, j] = 0.5
            if j + 1 < breadth:
                avg[j, j + 1] = 0.5
        elif j % NP == 0:
            avg[j, j] = 0.5
            if j > 0:
                avg[j, j - 1] = 0.5
    across = (avg @ deriv).T
    half = (0.5, 1.0, 1.0, 0.5)
    tables = []
    for pair, slots in enumerate(((0, 1, 2, 3, 4, 5), (2, 3, 4, 5, 6, 7))):
        out = np.zeros((6 * breadth, 2 * breadth))
        for col in range(2):
            j = 2 * pair + col
            for at, slot in enumerate(slots):
                if slot == SX_SLOT[j]:
                    block = half[j] * across
                elif slot in SY_SLOT:
                    block = half[j] * table[j, SY_SLOT.index(slot)] * avg.T
                else:
                    continue
                out[at * breadth : (at + 1) * breadth, col * breadth : (col + 1) * breadth] = block
        tables.append(out)
    return np.stack(tables).astype(np.float32)


def advect_kernel(
    n_face,
    n_elem,
    height,
    breadth,
    state_hbm,
    speed_ref,
    table_ref,
    final_hbm,
    inputs_ref,
    field,
    base,
    slots,
    raw,
    x_send,
    x_recv,
    y_send,
    y_recv,
    load_sem,
    store_sem,
    send_sem,
    recv_sem,
):
    feats = speed_ref.shape[0]
    size = feats // CHUNKS
    rows = size * height
    elements = height // NP
    face, elem = lax.axis_index("face"), lax.axis_index("elem")
    other = lax.rem(face + 1, n_face)
    right, left = lax.rem(elem + 1, n_elem), lax.rem(elem + n_elem - 1, n_elem)
    partners = ((face, left), (face, right), (other, left), (other, right), (other, elem))

    def load(chunk):
        at = pl.ds(chunk * rows, rows)
        return pltpu.make_async_copy(state_hbm.at[at], field.at[at], load_sem.at[chunk])

    def store(chunk):
        at = pl.ds(chunk * rows, rows)
        return pltpu.make_async_copy(field.at[at], final_hbm.at[at], store_sem.at[chunk])

    for chunk in range(CHUNKS):
        load(chunk).start()

    barrier = pltpu.get_barrier_semaphore()
    for partner in partners:
        pl.semaphore_signal(barrier, inc=1, device_id=partner, device_id_type=MESH)
    pl.semaphore_wait(barrier, len(partners))

    def copies(step):
        made = []
        for at in range(4):
            made.append(
                pltpu.make_async_remote_copy(
                    src_ref=x_send.at[step],
                    dst_ref=x_recv.at[step, at],
                    send_sem=send_sem.at[step, at],
                    recv_sem=recv_sem.at[step, at],
                    device_id=partners[at],
                    device_id_type=MESH,
                )
            )
        made.append(
            pltpu.make_async_remote_copy(
                src_ref=y_send.at[step],
                dst_ref=y_recv.at[step],
                send_sem=send_sem.at[step, 4],
                recv_sem=recv_sem.at[step, 4],
                device_id=partners[4],
                device_id_type=MESH,
            )
        )
        return made

    lane = lax.broadcasted_iota(jnp.int32, (16, breadth), 1)
    is_edge = (lane == 0) | (lane == breadth - 1)
    groups = 3
    trips = size // (16 * groups)

    def shift(y, group):
        return (2 * y + 1 + 2 * height * group) % breadth

    def speeds(chunk, at):
        pair = speed_ref[pl.ds(pl.multiple_of(chunk * size + at, 16), 16), :]
        across = jnp.broadcast_to(-pair[:, 0:1], (16, breadth))
        down = jnp.broadcast_to(-pair[:, 1:2], (16, breadth))
        return across, down

    def put_slots(at, y, value, across, down):
        element, j = divmod(y, NP)
        place = pl.ds(pl.multiple_of(element * size + at, 16), 16)
        sx, sy = SX_SLOT[j] * breadth, SY_SLOT[j] * breadth
        slots[place, sx : sx + breadth] = (across * value).astype(jnp.bfloat16)
        slots[place, sy : sy + breadth] = (down * value).astype(jnp.bfloat16)

    def field_at(chunk, at, y):
        return pl.ds((chunk * size + at) * height + y, 16, stride=height)

    def raw_at(chunk, at, y):
        element, j = divmod(y, NP)
        place = pl.ds(pl.multiple_of(element * size + at, 16), 16)
        return raw[chunk, j // 2, place, (j % 2) * breadth : (j % 2 + 1) * breadth]

    def prepare(chunk):
        @pl.loop(0, size // 16)
        def _(block):
            at = block * 16
            across, down = speeds(chunk, at)
            for y in range(height):
                put_slots(at, y, field[field_at(chunk, at, y), :], across, down)

    def apply_and_send(stage, chunk):
        step = stage * CHUNKS + chunk
        for pair in range(2):
            raw[chunk, pair] = jnp.dot(
                slots[:, 2 * pair * breadth : (2 * pair + 6) * breadth],
                table_ref[pair],
                preferred_element_type=jnp.float32,
            )
        y_send[step, 0] = raw[chunk, 0, 0:size, 0:breadth].astype(jnp.bfloat16)
        y_send[step, 1] = raw[
            chunk, 1, (elements - 1) * size : elements * size, breadth : 2 * breadth
        ].astype(jnp.bfloat16)

        @pl.loop(0, trips)
        def _(trip):
            packed = jnp.zeros((16, breadth), jnp.float32)
            for group in range(groups):
                at = (trip * groups + group) * 16
                for y in range(height):
                    turned = pltpu.roll(raw_at(chunk, at, y), shift(y, group), 1)
                    packed = jnp.where(lane // 2 == height * group + y, turned, packed)
            x_send[step, pl.ds(pl.multiple_of(trip * 16, 16), 16), :] = packed.astype(jnp.bfloat16)

        for copy in copies(step):
            copy.start()

    def finish(stage, chunk):
        step = stage * CHUNKS + chunk
        for copy in copies(step):
            copy.wait_recv()

        @pl.loop(0, trips)
        def _(trip):
            packed_at = pl.ds(pl.multiple_of(trip * 16, 16), 16)

            def merged(first):
                from_right = x_recv[step, first, packed_at, :].astype(jnp.float32)
                from_left = x_recv[step, first + 1, packed_at, :].astype(jnp.float32)
                return jnp.where(
                    lane % 2 == 0,
                    pltpu.roll(from_right, breadth - 1, 1),
                    pltpu.roll(from_left, 1, 1),
                )

            sides, corners = merged(0), merged(2)
            for group in range(groups):
                at = (trip * groups + group) * 16

                def edges(packed, y):
                    turned = pltpu.roll(packed, breadth - shift(y, group), 1)
                    return jnp.where(is_edge, turned, 0.0)

                def own(y):
                    return raw_at(chunk, at, y) + edges(sides, y)

                def across_face(row, y):
                    there = y_recv[step, row, pl.ds(pl.multiple_of(at, 16), 16), :]
                    return there.astype(jnp.float32) + edges(corners, y)

                across, down = speeds(chunk, at)

                def update(y, tendency):
                    kept = pl.ds(pl.multiple_of(chunk * size + at, 16), 16)
                    if stage == 0:
                        first = field[field_at(chunk, at, y), :]
                        base[y, kept, :] = first + 0.25 * tendency
                        value = first + tendency
                    elif stage == 1:
                        first = field[field_at(chunk, at, y), :]
                        value = base[y, kept, :] + 0.25 * tendency
                        base[y, kept, :] = first * (1.0 / 3.0) + value * (2.0 / 3.0)
                    else:
                        value = base[y, kept, :] + (2.0 / 3.0) * tendency
                        field[field_at(chunk, at, y), :] = value
                        half = (y % 2) * breadth
                        inputs_ref[y // 2, kept, half : half + breadth] = value.astype(
                            jnp.bfloat16
                        )
                        return
                    put_slots(at, y, value, across, down)

                for y in range(height):
                    if y == 0:
                        update(y, own(y) + across_face(1, height - 1))
                    elif y == height - 1:
                        update(y, own(y) + across_face(0, 0))
                    elif y % NP == NP - 1:
                        both = own(y) + own(y + 1)
                        update(y, both)
                        update(y + 1, both)
                    elif y % NP != 0:
                        update(y, own(y))

    @pl.loop(0, CHUNKS)
    def _(chunk):
        load(chunk).wait()
        prepare(chunk)
        apply_and_send(0, chunk)

    for stage in (1, 2):

        @pl.loop(0, CHUNKS)
        def _(chunk):
            finish(stage - 1, chunk)
            apply_and_send(stage, chunk)

    @pl.loop(0, CHUNKS)
    def _(chunk):
        finish(2, chunk)
        store(chunk).start()

    @pl.loop(0, 3 * CHUNKS)
    def _(step):
        for copy in copies(step):
            copy.wait_send()

    for chunk in range(CHUNKS):
        store(chunk).wait()


def physics_kernel(
    devices,
    final_hbm,
    inputs_ref,
    w_in,
    w_mid,
    w_top,
    w_out,
    bias_ref,
    span_ref,
    copied_hbm,
    tend_ref,
    parts_ref,
    outs,
    heat,
    copy_sem,
):
    pairs, _, width = inputs_ref.shape
    breadth = width // 2
    height = 2 * pairs
    n_out = w_out.shape[0]
    whole = pltpu.make_async_copy(final_hbm, copied_hbm, copy_sem)
    whole.start()

    def silu(value):
        half = 0.5 * value
        return (half + half * jnp.tanh(half)).astype(jnp.bfloat16)

    @pl.loop(0, pairs)
    def _(pair):
        hidden = inputs_ref[pair]
        for layer, weight in enumerate((w_in, w_mid, w_top)):
            hidden = silu(
                jnp.dot(weight[...], hidden, preferred_element_type=jnp.float32)
                + bias_ref[:, layer : layer + 1]
            )
        out = (
            jnp.dot(w_out[...], hidden, preferred_element_type=jnp.float32)
            + bias_ref[0:n_out, 3:4]
        )
        heat[pl.ds(pair, 1), :] = jnp.sum(out[:LEV], axis=0, keepdims=True)
        for side in range(2):
            outs[pl.ds(2 * pair + side, n_out, stride=height), :] = out[
                :, side * breadth : (side + 1) * breadth
            ]

    step = 15 * height

    @pl.loop(0, n_out * height // step)
    def _(block):
        at = pl.ds(pl.multiple_of(block * step, step), step)
        tend_ref[at, :] = outs[at, :].astype(jnp.bfloat16)

    @pl.loop(0, devices)
    def _(span):
        part = jnp.where(span_ref[...] == span, heat[...], 0.0)
        line = jnp.sum(part, axis=0, keepdims=True)
        parts_ref[span] = line[:, :breadth] + line[:, breadth:]

    whole.wait()


def local(tables, state, speed_x, speed_y, w_in, b_in, w_mid, b_mid, w_top, b_top, w_out, b_out, span_of):
    feats, height, breadth = state.shape
    n_face, n_elem = lax.axis_size("face"), lax.axis_size("elem")
    devices = n_face * n_elem
    size = feats // CHUNKS
    steps = 3 * CHUNKS
    vmem = pl.BlockSpec(memory_space=pltpu.VMEM)
    hbm = pl.BlockSpec(memory_space=pl.ANY)
    n_out, hidden = w_out.shape

    final, inputs = pl.pallas_call(
        functools.partial(advect_kernel, n_face, n_elem, height, breadth),
        out_shape=(
            jax.ShapeDtypeStruct((feats * height, breadth), jnp.float32),
            jax.ShapeDtypeStruct((height // 2, feats, 2 * breadth), jnp.bfloat16),
        ),
        in_specs=[hbm, vmem, vmem],
        out_specs=(hbm, vmem),
        scratch_shapes=[
            pltpu.VMEM((feats * height, breadth), jnp.float32),
            pltpu.VMEM((height, feats, breadth), jnp.float32),
            pltpu.VMEM((height // NP * size, 8 * breadth), jnp.bfloat16),
            pltpu.VMEM((CHUNKS, 2, height // NP * size, 2 * breadth), jnp.float32),
            pltpu.VMEM((steps, size // 3, breadth), jnp.bfloat16),
            pltpu.VMEM((steps, 4, size // 3, breadth), jnp.bfloat16),
            pltpu.VMEM((steps, 2, size, breadth), jnp.bfloat16),
            pltpu.VMEM((steps, 2, size, breadth), jnp.bfloat16),
            pltpu.SemaphoreType.DMA((CHUNKS,)),
            pltpu.SemaphoreType.DMA((CHUNKS,)),
            pltpu.SemaphoreType.DMA((steps, 5)),
            pltpu.SemaphoreType.DMA((steps, 5)),
        ],
        compiler_params=pltpu.CompilerParams(
            collective_id=0, has_side_effects=True, vmem_limit_bytes=44 * 2**20
        ),
        name="advect",
    )(state.reshape(feats * height, breadth), jnp.stack([speed_x, speed_y], axis=1), tables)

    bias = jnp.stack([b_in, b_mid, b_top, jnp.pad(b_out, (0, hidden - n_out))], axis=1)
    final, tend, parts = pl.pallas_call(
        functools.partial(physics_kernel, devices),
        out_shape=(
            jax.ShapeDtypeStruct((feats * height, breadth), jnp.float32),
            jax.ShapeDtypeStruct((n_out * height, breadth), jnp.bfloat16),
            jax.ShapeDtypeStruct((devices, 1, breadth), jnp.float32),
        ),
        in_specs=[hbm] + [vmem] * 7,
        out_specs=(hbm, vmem, vmem),
        scratch_shapes=[
            pltpu.VMEM((n_out * height, breadth), jnp.float32),
            pltpu.VMEM((height // 2, 2 * breadth), jnp.float32),
            pltpu.SemaphoreType.DMA,
        ],
        compiler_params=pltpu.CompilerParams(vmem_limit_bytes=44 * 2**20),
        name="physics",
    )(
        final,
        inputs,
        w_in,
        w_mid,
        w_top,
        w_out,
        bias,
        span_of.reshape(height // 2, 2 * breadth),
    )
    totals = jnp.sum(parts, axis=(1, 2))
    span_heating = lax.psum_scatter(totals, ("face", "elem"), scatter_dimension=0, tiled=True) / (
        height * breadth
    )
    return (
        final.reshape(state.shape),
        tend.reshape(n_out, height, breadth),
        span_heating,
    )


def solution(mesh):
    specs = (
        (P(None, "face", "elem"),) + (P(),) * 10 + (P("face", "elem", None, None),)
    )
    inner = jax.shard_map(
        local,
        mesh=mesh,
        in_specs=(P(),) + specs,
        out_specs=(P(None, "face", "elem"), P(None, "face", "elem"), P(("face", "elem"))),
        check_vma=False,
    )

    def whole(state, *rest):
        breadth = state.shape[2] // mesh.shape["elem"]
        tables = jnp.asarray(operator_tables(breadth), dtype=jnp.bfloat16)
        return inner(tables, state, *rest)

    return whole
```

```python
import functools
import math

import jax
import jax.numpy as jnp
import numpy as np
from jax import lax
from jax.experimental import pallas as pl
from jax.experimental.pallas import tpu as pltpu
from jax.sharding import PartitionSpec as P

NP = 4
LEV = 72
CHUNKS = 3
MESH = pl.DeviceIdType.MESH
SX_SLOT = (0, 1, 6, 7)
SY_SLOT = (2, 3, 4, 5)


def gll_matrix():
    inner_node = 1.0 / math.sqrt(5.0)
    nodes = np.array([-1.0, -inner_node, inner_node, 1.0])
    weights = np.array(
        [1.0 / np.prod([nodes[j] - nodes[k] for k in range(4) if k != j]) for j in range(4)]
    )
    matrix = np.zeros((4, 4))
    for i in range(4):
        for j in range(4):
            if i != j:
                matrix[i, j] = weights[j] / weights[i] / (nodes[i] - nodes[j])
    for i in range(4):
        matrix[i, i] = -np.sum(matrix[i])
    return matrix


def operator_tables(breadth):
    table = gll_matrix()
    deriv = np.kron(np.eye(breadth // NP), table)
    avg = np.eye(breadth)
    for j in range(breadth):
        if j % NP == NP - 1:
            avg[j, j] = 0.5
            if j + 1 < breadth:
                avg[j, j + 1] = 0.5
        elif j % NP == 0:
            avg[j, j] = 0.5
            if j > 0:
                avg[j, j - 1] = 0.5
    across = (avg @ deriv).T
    half = (0.5, 1.0, 1.0, 0.5)
    tables = []
    for pair, slots in enumerate(((0, 1, 2, 3, 4, 5), (2, 3, 4, 5, 6, 7))):
        out = np.zeros((6 * breadth, 2 * breadth))
        for col in range(2):
            j = 2 * pair + col
            for at, slot in enumerate(slots):
                if slot == SX_SLOT[j]:
                    block = half[j] * across
                elif slot in SY_SLOT:
                    block = half[j] * table[j, SY_SLOT.index(slot)] * avg.T
                else:
                    continue
                out[at * breadth : (at + 1) * breadth, col * breadth : (col + 1) * breadth] = block
        tables.append(out)
    return np.stack(tables).astype(np.float32)


def edge_tables(breadth):
    pick = np.zeros((NP * breadth, 2 * breadth), np.float32)
    place = np.zeros((breadth, NP * breadth), np.float32)
    for lane in range(breadth):
        j, side = divmod(lane % (2 * NP), 2)
        edge = 0 if side else breadth - 1
        pick[j * breadth + edge, lane] = 1.0
        pick[(NP - 1 - j) * breadth + edge, breadth + lane] = 1.0
        place[lane, j * breadth + (breadth - 1 if side else 0)] = 1.0
    return pick, place


def advect_kernel(
    n_face,
    n_elem,
    height,
    breadth,
    state_hbm,
    speed_ref,
    table_ref,
    pick_ref,
    place_ref,
    final_hbm,
    inputs_ref,
    field,
    base,
    slots,
    raw,
    rows16,
    edged,
    x_send,
    x_recv,
    y_send,
    y_recv,
    load_sem,
    store_sem,
    send_sem,
    recv_sem,
):
    feats = speed_ref.shape[0]
    size = feats // CHUNKS
    rows = size * height
    elements = height // NP
    face, elem = lax.axis_index("face"), lax.axis_index("elem")
    other = lax.rem(face + 1, n_face)
    right, left = lax.rem(elem + 1, n_elem), lax.rem(elem + n_elem - 1, n_elem)
    partners = ((face, left), (face, right), (other, left), (other, right), (other, elem))

    def load(chunk):
        at = pl.ds(chunk * rows, rows)
        return pltpu.make_async_copy(state_hbm.at[at], field.at[at], load_sem.at[chunk])

    def store(chunk):
        at = pl.ds(chunk * rows, rows)
        return pltpu.make_async_copy(field.at[at], final_hbm.at[at], store_sem.at[chunk])

    for chunk in range(CHUNKS):
        load(chunk).start()

    barrier = pltpu.get_barrier_semaphore()
    for partner in partners:
        pl.semaphore_signal(barrier, inc=1, device_id=partner, device_id_type=MESH)
    pl.semaphore_wait(barrier, len(partners))

    def copies(step):
        made = []
        for at in range(4):
            made.append(
                pltpu.make_async_remote_copy(
                    src_ref=x_send.at[step, at // 2],
                    dst_ref=x_recv.at[step, at],
                    send_sem=send_sem.at[step, at],
                    recv_sem=recv_sem.at[step, at],
                    device_id=partners[at],
                    device_id_type=MESH,
                )
            )
        made.append(
            pltpu.make_async_remote_copy(
                src_ref=y_send.at[step],
                dst_ref=y_recv.at[step],
                send_sem=send_sem.at[step, 4],
                recv_sem=recv_sem.at[step, 4],
                device_id=partners[4],
                device_id_type=MESH,
            )
        )
        return made

    lane = lax.broadcasted_iota(jnp.int32, (16, breadth), 1)
    groups = 3
    trips = size // (16 * groups)

    def speeds(chunk, at):
        pair = speed_ref[pl.ds(pl.multiple_of(chunk * size + at, 16), 16), :]
        across = jnp.broadcast_to(-pair[:, 0:1], (16, breadth))
        down = jnp.broadcast_to(-pair[:, 1:2], (16, breadth))
        return across, down

    def put_slots(at, y, value, across, down):
        element, j = divmod(y, NP)
        place = pl.ds(pl.multiple_of(element * size + at, 16), 16)
        sx, sy = SX_SLOT[j] * breadth, SY_SLOT[j] * breadth
        slots[place, sx : sx + breadth] = (across * value).astype(jnp.bfloat16)
        slots[place, sy : sy + breadth] = (down * value).astype(jnp.bfloat16)

    def field_at(chunk, at, y):
        return pl.ds((chunk * size + at) * height + y, 16, stride=height)

    def raw_at(chunk, at, y):
        element, j = divmod(y, NP)
        place = pl.ds(pl.multiple_of(element * size + at, 16), 16)
        return raw[chunk, j // 2, place, (j % 2) * breadth : (j % 2 + 1) * breadth]

    def prepare(chunk):
        @pl.loop(0, size // 16)
        def _(block):
            at = block * 16
            across, down = speeds(chunk, at)
            for y in range(height):
                put_slots(at, y, field[field_at(chunk, at, y), :], across, down)

    def apply_and_send(stage, chunk):
        step = stage * CHUNKS + chunk
        for pair in range(2):
            raw[chunk, pair] = jnp.dot(
                slots[:, 2 * pair * breadth : (2 * pair + 6) * breadth],
                table_ref[pair],
                preferred_element_type=jnp.float32,
            )
        y_send[step, 0] = raw[chunk, 0, 0:size, 0:breadth].astype(jnp.bfloat16)
        y_send[step, 1] = raw[
            chunk, 1, (elements - 1) * size : elements * size, breadth : 2 * breadth
        ].astype(jnp.bfloat16)

        for pair in range(2):
            rows16[:, 2 * pair * breadth : 2 * (pair + 1) * breadth] = raw[chunk, pair].astype(
                jnp.bfloat16
            )
        edged[:, 0 : 2 * breadth] = jnp.dot(
            rows16[...], pick_ref[...], preferred_element_type=jnp.float32
        )

        @pl.loop(0, trips)
        def _(trip):
            for kind in range(2):
                packed = jnp.zeros((16, breadth), jnp.float32)
                for group in range(groups):
                    at = (trip * groups + group) * 16
                    for element in range(elements):
                        there = edged[
                            pl.ds(pl.multiple_of(element * size + at, 16), 16),
                            kind * breadth : (kind + 1) * breadth,
                        ]
                        spot = elements - 1 - element if kind else element
                        packed = jnp.where(
                            lane // (2 * NP) == elements * group + spot, there, packed
                        )
                x_send[step, kind, pl.ds(pl.multiple_of(trip * 16, 16), 16), :] = packed.astype(
                    jnp.bfloat16
                )

        for copy in copies(step):
            copy.start()

    def finish(stage, chunk):
        step = stage * CHUNKS + chunk
        for copy in copies(step):
            copy.wait_recv()

        @pl.loop(0, trips)
        def _(trip):
            packed_at = pl.ds(pl.multiple_of(trip * 16, 16), 16)

            def merged(first):
                from_right = x_recv[step, first, packed_at, :].astype(jnp.float32)
                from_left = x_recv[step, first + 1, packed_at, :].astype(jnp.float32)
                return jnp.where(lane % 2 == 0, from_left, from_right)

            y_of = lane // 2 % height
            outer = (y_of == 0) | (y_of == height - 1)
            total = merged(0) + jnp.where(outer, merged(2), 0.0)
            for group in range(groups):
                at = (trip * groups + group) * 16
                for element in range(elements):
                    own_lanes = lane // (2 * NP) == elements * group + element
                    rows16[pl.ds(pl.multiple_of(element * size + at, 16), 16), 0:breadth] = (
                        jnp.where(own_lanes, total, 0.0).astype(jnp.bfloat16)
                    )

        edged[...] = jnp.dot(
            rows16[:, 0:breadth], place_ref[...], preferred_element_type=jnp.float32
        )

        @pl.loop(0, trips)
        def _(trip):
            for group in range(groups):
                at = (trip * groups + group) * 16

                def own(y):
                    element, j = divmod(y, NP)
                    added = edged[
                        pl.ds(pl.multiple_of(element * size + at, 16), 16),
                        j * breadth : (j + 1) * breadth,
                    ]
                    return raw_at(chunk, at, y) + added

                def across_face(row):
                    there = y_recv[step, row, pl.ds(pl.multiple_of(at, 16), 16), :]
                    return there.astype(jnp.float32)

                across, down = speeds(chunk, at)

                def update(y, tendency):
                    kept = pl.ds(pl.multiple_of(chunk * size + at, 16), 16)
                    if stage == 0:
                        first = field[field_at(chunk, at, y), :]
                        base[y, kept, :] = first + 0.25 * tendency
                        value = first + tendency
                    elif stage == 1:
                        first = field[field_at(chunk, at, y), :]
                        value = base[y, kept, :] + 0.25 * tendency
                        base[y, kept, :] = first * (1.0 / 3.0) + value * (2.0 / 3.0)
                    else:
                        value = base[y, kept, :] + (2.0 / 3.0) * tendency
                        field[field_at(chunk, at, y), :] = value
                        half = (y % 2) * breadth
                        inputs_ref[y // 2, kept, half : half + breadth] = value.astype(
                            jnp.bfloat16
                        )
                        return
                    put_slots(at, y, value, across, down)

                for y in range(height):
                    if y == 0:
                        update(y, own(y) + across_face(1))
                    elif y == height - 1:
                        update(y, own(y) + across_face(0))
                    elif y % NP == NP - 1:
                        both = own(y) + own(y + 1)
                        update(y, both)
                        update(y + 1, both)
                    elif y % NP != 0:
                        update(y, own(y))

    @pl.loop(0, CHUNKS)
    def _(chunk):
        load(chunk).wait()
        prepare(chunk)
        apply_and_send(0, chunk)

    for stage in (1, 2):

        @pl.loop(0, CHUNKS)
        def _(chunk):
            finish(stage - 1, chunk)
            apply_and_send(stage, chunk)

    @pl.loop(0, CHUNKS)
    def _(chunk):
        finish(2, chunk)
        store(chunk).start()

    @pl.loop(0, 3 * CHUNKS)
    def _(step):
        for copy in copies(step):
            copy.wait_send()

    for chunk in range(CHUNKS):
        store(chunk).wait()


def physics_kernel(
    devices,
    final_hbm,
    inputs_ref,
    w_in,
    w_mid,
    w_top,
    w_out,
    bias_ref,
    span_ref,
    copied_hbm,
    tend_ref,
    parts_ref,
    outs,
    heat,
    copy_sem,
):
    pairs, _, width = inputs_ref.shape
    breadth = width // 2
    height = 2 * pairs
    n_out = w_out.shape[0]
    whole = pltpu.make_async_copy(final_hbm, copied_hbm, copy_sem)
    whole.start()

    def silu(value):
        half = 0.5 * value
        return (half + half * jnp.tanh(half)).astype(jnp.bfloat16)

    @pl.loop(0, pairs)
    def _(pair):
        hidden = inputs_ref[pair]
        for layer, weight in enumerate((w_in, w_mid, w_top)):
            hidden = silu(
                jnp.dot(weight[...], hidden, preferred_element_type=jnp.float32)
                + bias_ref[:, layer : layer + 1]
            )
        out = (
            jnp.dot(w_out[...], hidden, preferred_element_type=jnp.float32)
            + bias_ref[0:n_out, 3:4]
        )
        heat[pl.ds(pair, 1), :] = jnp.sum(out[:LEV], axis=0, keepdims=True)
        for side in range(2):
            outs[pl.ds(2 * pair + side, n_out, stride=height), :] = out[
                :, side * breadth : (side + 1) * breadth
            ]

    step = 15 * height

    @pl.loop(0, n_out * height // step)
    def _(block):
        at = pl.ds(pl.multiple_of(block * step, step), step)
        tend_ref[at, :] = outs[at, :].astype(jnp.bfloat16)

    @pl.loop(0, devices)
    def _(span):
        part = jnp.where(span_ref[...] == span, heat[...], 0.0)
        line = jnp.sum(part, axis=0, keepdims=True)
        parts_ref[span] = line[:, :breadth] + line[:, breadth:]

    whole.wait()


def totals_kernel(n_face, n_elem, columns, parts_ref, out_ref, held, send_sem, recv_sem):
    devices = n_face * n_elem
    me = lax.axis_index("face") * n_elem + lax.axis_index("elem")
    barrier = pltpu.get_barrier_semaphore()

    def place(number):
        return (number // n_elem, number % n_elem)

    def copy(step):
        target = lax.rem(me + step, devices)
        return pltpu.make_async_remote_copy(
            src_ref=parts_ref.at[target],
            dst_ref=held.at[step],
            send_sem=send_sem.at[step],
            recv_sem=recv_sem.at[step],
            device_id=place(target),
            device_id_type=MESH,
        )

    @pl.loop(1, devices)
    def _(step):
        pl.semaphore_signal(
            barrier, inc=1, device_id=place(lax.rem(me + step, devices)), device_id_type=MESH
        )

    pl.semaphore_wait(barrier, devices - 1)

    @pl.loop(1, devices)
    def _(step):
        copy(step).start()

    held[0] = parts_ref[me]

    @pl.loop(1, devices)
    def _(step):
        copy(step).wait_recv()

    out_ref[0] = jnp.sum(held[...]) / columns

    @pl.loop(1, devices)
    def _(step):
        copy(step).wait_send()


def local(tables, state, speed_x, speed_y, w_in, b_in, w_mid, b_mid, w_top, b_top, w_out, b_out, span_of):
    feats, height, breadth = state.shape
    n_face, n_elem = lax.axis_size("face"), lax.axis_size("elem")
    devices = n_face * n_elem
    size = feats // CHUNKS
    steps = 3 * CHUNKS
    vmem = pl.BlockSpec(memory_space=pltpu.VMEM)
    hbm = pl.BlockSpec(memory_space=pl.ANY)
    n_out, hidden = w_out.shape

    final, inputs = pl.pallas_call(
        functools.partial(advect_kernel, n_face, n_elem, height, breadth),
        out_shape=(
            jax.ShapeDtypeStruct((feats * height, breadth), jnp.float32),
            jax.ShapeDtypeStruct((height // 2, feats, 2 * breadth), jnp.bfloat16),
        ),
        in_specs=[hbm, vmem, vmem, vmem, vmem],
        out_specs=(hbm, vmem),
        scratch_shapes=[
            pltpu.VMEM((feats * height, breadth), jnp.float32),
            pltpu.VMEM((height, feats, breadth), jnp.float32),
            pltpu.VMEM((height // NP * size, 8 * breadth), jnp.bfloat16),
            pltpu.VMEM((CHUNKS, 2, height // NP * size, 2 * breadth), jnp.float32),
            pltpu.VMEM((height // NP * size, NP * breadth), jnp.bfloat16),
            pltpu.VMEM((height // NP * size, NP * breadth), jnp.float32),
            pltpu.VMEM((steps, 2, size // 3, breadth), jnp.bfloat16),
            pltpu.VMEM((steps, 4, size // 3, breadth), jnp.bfloat16),
            pltpu.VMEM((steps, 2, size, breadth), jnp.bfloat16),
            pltpu.VMEM((steps, 2, size, breadth), jnp.bfloat16),
            pltpu.SemaphoreType.DMA((CHUNKS,)),
            pltpu.SemaphoreType.DMA((CHUNKS,)),
            pltpu.SemaphoreType.DMA((steps, 5)),
            pltpu.SemaphoreType.DMA((steps, 5)),
        ],
        compiler_params=pltpu.CompilerParams(
            collective_id=0, has_side_effects=True, vmem_limit_bytes=60 * 2**20
        ),
        name="advect",
    )(state.reshape(feats * height, breadth), jnp.stack([speed_x, speed_y], axis=1), *tables)

    bias = jnp.stack([b_in, b_mid, b_top, jnp.pad(b_out, (0, hidden - n_out))], axis=1)
    final, tend, parts = pl.pallas_call(
        functools.partial(physics_kernel, devices),
        out_shape=(
            jax.ShapeDtypeStruct((feats * height, breadth), jnp.float32),
            jax.ShapeDtypeStruct((n_out * height, breadth), jnp.bfloat16),
            jax.ShapeDtypeStruct((devices, 1, breadth), jnp.float32),
        ),
        in_specs=[hbm] + [vmem] * 7,
        out_specs=(hbm, vmem, vmem),
        scratch_shapes=[
            pltpu.VMEM((n_out * height, breadth), jnp.float32),
            pltpu.VMEM((height // 2, 2 * breadth), jnp.float32),
            pltpu.SemaphoreType.DMA,
        ],
        compiler_params=pltpu.CompilerParams(vmem_limit_bytes=60 * 2**20),
        name="physics",
    )(
        final,
        inputs,
        w_in,
        w_mid,
        w_top,
        w_out,
        bias,
        span_of.reshape(height // 2, 2 * breadth),
    )
    span_heating = pl.pallas_call(
        functools.partial(totals_kernel, n_face, n_elem, height * breadth),
        out_shape=jax.ShapeDtypeStruct((1,), jnp.float32),
        in_specs=[vmem],
        out_specs=pl.BlockSpec(memory_space=pltpu.SMEM),
        scratch_shapes=[
            pltpu.VMEM((devices, 1, breadth), jnp.float32),
            pltpu.SemaphoreType.DMA((devices,)),
            pltpu.SemaphoreType.DMA((devices,)),
        ],
        compiler_params=pltpu.CompilerParams(collective_id=1, has_side_effects=True),
        name="totals",
    )(parts)
    return (
        final.reshape(state.shape),
        tend.reshape(n_out, height, breadth),
        span_heating,
    )


def solution(mesh):
    specs = (
        (P(None, "face", "elem"),) + (P(),) * 10 + (P("face", "elem", None, None),)
    )
    inner = jax.shard_map(
        local,
        mesh=mesh,
        in_specs=((P(), P(), P()),) + specs,
        out_specs=(P(None, "face", "elem"), P(None, "face", "elem"), P(("face", "elem"))),
        check_vma=False,
    )

    def whole(state, *rest):
        breadth = state.shape[2] // mesh.shape["elem"]
        made = (operator_tables(breadth),) + edge_tables(breadth)
        tables = tuple(jnp.asarray(table, dtype=jnp.bfloat16) for table in made)
        return inner(tables, state, *rest)

    return whole
```

```python
import functools
import math

import jax
import jax.numpy as jnp
import numpy as np
from jax import lax
from jax.experimental import pallas as pl
from jax.experimental.pallas import tpu as pltpu
from jax.sharding import PartitionSpec as P

NP = 4
LEV = 72
CHUNKS = 3
MESH = pl.DeviceIdType.MESH
SX_SLOT = (0, 1, 6, 7)
SY_SLOT = (2, 3, 4, 5)


def gll_matrix():
    inner_node = 1.0 / math.sqrt(5.0)
    nodes = np.array([-1.0, -inner_node, inner_node, 1.0])
    weights = np.array(
        [1.0 / np.prod([nodes[j] - nodes[k] for k in range(4) if k != j]) for j in range(4)]
    )
    matrix = np.zeros((4, 4))
    for i in range(4):
        for j in range(4):
            if i != j:
                matrix[i, j] = weights[j] / weights[i] / (nodes[i] - nodes[j])
    for i in range(4):
        matrix[i, i] = -np.sum(matrix[i])
    return matrix


def operator_tables(breadth):
    table = gll_matrix()
    deriv = np.kron(np.eye(breadth // NP), table)
    avg = np.eye(breadth)
    for j in range(breadth):
        if j % NP == NP - 1:
            avg[j, j] = 0.5
            if j + 1 < breadth:
                avg[j, j + 1] = 0.5
        elif j % NP == 0:
            avg[j, j] = 0.5
            if j > 0:
                avg[j, j - 1] = 0.5
    across = (avg @ deriv).T
    half = (0.5, 1.0, 1.0, 0.5)
    tables = []
    for pair, slots in enumerate(((0, 1, 2, 3, 4, 5), (2, 3, 4, 5, 6, 7))):
        out = np.zeros((6 * breadth, 2 * breadth))
        for col in range(2):
            j = 2 * pair + col
            for at, slot in enumerate(slots):
                if slot == SX_SLOT[j]:
                    block = half[j] * across
                elif slot in SY_SLOT:
                    block = half[j] * table[j, SY_SLOT.index(slot)] * avg.T
                else:
                    continue
                out[at * breadth : (at + 1) * breadth, col * breadth : (col + 1) * breadth] = block
        tables.append(out)
    return np.stack(tables).astype(np.float32)


def edge_tables(breadth):
    pick = np.zeros((NP * breadth, 2 * breadth), np.float32)
    place = np.zeros((breadth, NP * breadth), np.float32)
    for lane in range(breadth):
        j, side = divmod(lane % (2 * NP), 2)
        edge = 0 if side else breadth - 1
        pick[j * breadth + edge, lane] = 1.0
        pick[(NP - 1 - j) * breadth + edge, breadth + lane] = 1.0
        place[lane, j * breadth + (breadth - 1 if side else 0)] = 1.0
    return pick, place


def advect_kernel(
    n_face,
    n_elem,
    height,
    breadth,
    state_hbm,
    speed_ref,
    table_ref,
    pick_ref,
    place_ref,
    final_hbm,
    inputs_ref,
    field,
    base,
    slots,
    raw,
    rows16,
    edged,
    x_send,
    x_recv,
    y_send,
    y_recv,
    load_sem,
    store_sem,
    send_sem,
    recv_sem,
):
    feats = speed_ref.shape[0]
    size = feats // CHUNKS
    rows = size * height
    elements = height // NP
    face, elem = lax.axis_index("face"), lax.axis_index("elem")
    other = lax.rem(face + 1, n_face)
    right, left = lax.rem(elem + 1, n_elem), lax.rem(elem + n_elem - 1, n_elem)
    partners = ((face, left), (face, right), (other, left), (other, right), (other, elem))

    def load(chunk):
        at = pl.ds(chunk * rows, rows)
        return pltpu.make_async_copy(state_hbm.at[at], field.at[at], load_sem.at[chunk])

    def store(chunk):
        at = pl.ds(chunk * rows, rows)
        return pltpu.make_async_copy(field.at[at], final_hbm.at[at], store_sem.at[chunk])

    for chunk in range(CHUNKS):
        load(chunk).start()

    barrier = pltpu.get_barrier_semaphore()
    for partner in partners:
        pl.semaphore_signal(barrier, inc=1, device_id=partner, device_id_type=MESH)
    pl.semaphore_wait(barrier, len(partners))

    def copies(step):
        made = []
        for at in range(4):
            made.append(
                pltpu.make_async_remote_copy(
                    src_ref=x_send.at[step, at // 2],
                    dst_ref=x_recv.at[step, at],
                    send_sem=send_sem.at[step, at],
                    recv_sem=recv_sem.at[step, at],
                    device_id=partners[at],
                    device_id_type=MESH,
                )
            )
        made.append(
            pltpu.make_async_remote_copy(
                src_ref=y_send.at[step],
                dst_ref=y_recv.at[step],
                send_sem=send_sem.at[step, 4],
                recv_sem=recv_sem.at[step, 4],
                device_id=partners[4],
                device_id_type=MESH,
            )
        )
        return made

    lane = lax.broadcasted_iota(jnp.int32, (16, breadth), 1)
    groups = 3
    trips = size // (16 * groups)

    def speeds(chunk, at):
        pair = speed_ref[pl.ds(pl.multiple_of(chunk * size + at, 16), 16), :]
        across = jnp.broadcast_to(-pair[:, 0:1], (16, breadth))
        down = jnp.broadcast_to(-pair[:, 1:2], (16, breadth))
        return across, down

    def put_slots(at, y, value, across, down):
        element, j = divmod(y, NP)
        place = pl.ds(pl.multiple_of(element * size + at, 16), 16)
        sx, sy = SX_SLOT[j] * breadth, SY_SLOT[j] * breadth
        slots[place, sx : sx + breadth] = (across * value).astype(jnp.bfloat16)
        slots[place, sy : sy + breadth] = (down * value).astype(jnp.bfloat16)

    def field_at(chunk, at, y):
        return pl.ds((chunk * size + at) * height + y, 16, stride=height)

    def raw_at(chunk, at, y):
        element, j = divmod(y, NP)
        place = pl.ds(pl.multiple_of(element * size + at, 16), 16)
        return raw[chunk, j // 2, place, (j % 2) * breadth : (j % 2 + 1) * breadth]

    def prepare(chunk):
        @pl.loop(0, size // 16)
        def _(block):
            at = block * 16
            across, down = speeds(chunk, at)
            for y in range(height):
                put_slots(at, y, field[field_at(chunk, at, y), :], across, down)

    def apply_and_send(stage, chunk):
        step = stage * CHUNKS + chunk
        for pair in range(2):
            raw[chunk, pair] = jnp.dot(
                slots[:, 2 * pair * breadth : (2 * pair + 6) * breadth],
                table_ref[pair],
                preferred_element_type=jnp.float32,
            )
        y_send[step, 0] = raw[chunk, 0, 0:size, 0:breadth].astype(jnp.bfloat16)
        y_send[step, 1] = raw[
            chunk, 1, (elements - 1) * size : elements * size, breadth : 2 * breadth
        ].astype(jnp.bfloat16)

        for pair in range(2):
            rows16[:, 2 * pair * breadth : 2 * (pair + 1) * breadth] = raw[chunk, pair].astype(
                jnp.bfloat16
            )
        edged[:, 0 : 2 * breadth] = jnp.dot(
            rows16[...], pick_ref[...], preferred_element_type=jnp.float32
        )

        @pl.loop(0, trips)
        def _(trip):
            for kind in range(2):
                packed = jnp.zeros((16, breadth), jnp.float32)
                for group in range(groups):
                    at = (trip * groups + group) * 16
                    for element in range(elements):
                        there = edged[
                            pl.ds(pl.multiple_of(element * size + at, 16), 16),
                            kind * breadth : (kind + 1) * breadth,
                        ]
                        spot = elements - 1 - element if kind else element
                        packed = jnp.where(
                            lane // (2 * NP) == elements * group + spot, there, packed
                        )
                x_send[step, kind, pl.ds(pl.multiple_of(trip * 16, 16), 16), :] = packed.astype(
                    jnp.bfloat16
                )

        for copy in copies(step):
            copy.start()

    def finish(stage, chunk):
        step = stage * CHUNKS + chunk
        for copy in copies(step):
            copy.wait_recv()

        @pl.loop(0, trips)
        def _(trip):
            packed_at = pl.ds(pl.multiple_of(trip * 16, 16), 16)

            def merged(first):
                from_right = x_recv[step, first, packed_at, :].astype(jnp.float32)
                from_left = x_recv[step, first + 1, packed_at, :].astype(jnp.float32)
                return jnp.where(lane % 2 == 0, from_left, from_right)

            y_of = lane // 2 % height
            outer = (y_of == 0) | (y_of == height - 1)
            total = merged(0) + jnp.where(outer, merged(2), 0.0)
            for group in range(groups):
                at = (trip * groups + group) * 16
                for element in range(elements):
                    own_lanes = lane // (2 * NP) == elements * group + element
                    rows16[pl.ds(pl.multiple_of(element * size + at, 16), 16), 0:breadth] = (
                        jnp.where(own_lanes, total, 0.0).astype(jnp.bfloat16)
                    )

        edged[...] = jnp.dot(
            rows16[:, 0:breadth], place_ref[...], preferred_element_type=jnp.float32
        )

        @pl.loop(0, trips)
        def _(trip):
            for group in range(groups):
                at = (trip * groups + group) * 16

                def own(y):
                    element, j = divmod(y, NP)
                    added = edged[
                        pl.ds(pl.multiple_of(element * size + at, 16), 16),
                        j * breadth : (j + 1) * breadth,
                    ]
                    return raw_at(chunk, at, y) + added

                def across_face(row):
                    there = y_recv[step, row, pl.ds(pl.multiple_of(at, 16), 16), :]
                    return there.astype(jnp.float32)

                across, down = speeds(chunk, at)

                def update(y, tendency):
                    kept = pl.ds(pl.multiple_of(chunk * size + at, 16), 16)
                    if stage == 0:
                        first = field[field_at(chunk, at, y), :]
                        base[y, kept, :] = first + 0.25 * tendency
                        value = first + tendency
                    elif stage == 1:
                        first = field[field_at(chunk, at, y), :]
                        value = base[y, kept, :] + 0.25 * tendency
                        base[y, kept, :] = first * (1.0 / 3.0) + value * (2.0 / 3.0)
                    else:
                        value = base[y, kept, :] + (2.0 / 3.0) * tendency
                        field[field_at(chunk, at, y), :] = value
                        half = (y % 2) * breadth
                        inputs_ref[y // 2, kept, half : half + breadth] = value.astype(
                            jnp.bfloat16
                        )
                        return
                    put_slots(at, y, value, across, down)

                for y in range(height):
                    if y == 0:
                        update(y, own(y) + across_face(1))
                    elif y == height - 1:
                        update(y, own(y) + across_face(0))
                    elif y % NP == NP - 1:
                        both = own(y) + own(y + 1)
                        update(y, both)
                        update(y + 1, both)
                    elif y % NP != 0:
                        update(y, own(y))

    @pl.loop(0, CHUNKS)
    def _(chunk):
        load(chunk).wait()
        prepare(chunk)
        apply_and_send(0, chunk)

    for stage in (1, 2):

        @pl.loop(0, CHUNKS)
        def _(chunk):
            finish(stage - 1, chunk)
            apply_and_send(stage, chunk)

    @pl.loop(0, CHUNKS)
    def _(chunk):
        finish(2, chunk)
        store(chunk).start()

    @pl.loop(0, 3 * CHUNKS)
    def _(step):
        for copy in copies(step):
            copy.wait_send()

    for chunk in range(CHUNKS):
        store(chunk).wait()


def physics_kernel(
    devices,
    final_hbm,
    inputs_ref,
    w_in,
    w_mid,
    w_top,
    w_out,
    bias_ref,
    span_ref,
    copied_hbm,
    tend_ref,
    parts_ref,
    outs,
    heat,
    spans,
    staged,
    copy_sem,
):
    pairs, _, width = inputs_ref.shape
    breadth = width // 2
    height = 2 * pairs
    n_out = w_out.shape[0]
    fetch = pltpu.make_async_copy(final_hbm, staged, copy_sem.at[0])
    write = pltpu.make_async_copy(staged, copied_hbm, copy_sem.at[1])
    fetch.start()
    for pair in range(pairs):
        spans[pair : pair + 1, :] = span_ref[:, pair * width : (pair + 1) * width]

    def silu(value):
        half = 0.5 * value
        return (half + half * jnp.tanh(half)).astype(jnp.bfloat16)

    def columns(pair):
        hidden = inputs_ref[pair]
        for layer, weight in enumerate((w_in, w_mid, w_top)):
            hidden = silu(
                jnp.dot(weight[...], hidden, preferred_element_type=jnp.float32)
                + bias_ref[:, layer : layer + 1]
            )
        out = (
            jnp.dot(w_out[...], hidden, preferred_element_type=jnp.float32)
            + bias_ref[0:n_out, 3:4]
        )
        heat[pl.ds(pair, 1), :] = jnp.sum(out[:LEV], axis=0, keepdims=True)
        for side in range(2):
            outs[pl.ds(2 * pair + side, n_out, stride=height), :] = out[
                :, side * breadth : (side + 1) * breadth
            ]

    pl.loop(0, pairs // 2)(columns)
    fetch.wait()
    write.start()
    pl.loop(pairs // 2, pairs)(columns)

    step = 15 * height

    @pl.loop(0, n_out * height // step)
    def _(block):
        at = pl.ds(pl.multiple_of(block * step, step), step)
        tend_ref[at, :] = outs[at, :].astype(jnp.bfloat16)

    @pl.loop(0, devices)
    def _(span):
        part = jnp.where(spans[...] == span, heat[...], 0.0)
        line = jnp.sum(part, axis=0, keepdims=True)
        parts_ref[span] = line[:, :breadth] + line[:, breadth:]

    write.wait()


def totals_kernel(n_face, n_elem, columns, parts_ref, out_ref, held, send_sem, recv_sem):
    devices = n_face * n_elem
    me = lax.axis_index("face") * n_elem + lax.axis_index("elem")
    barrier = pltpu.get_barrier_semaphore()

    def place(number):
        return (number // n_elem, number % n_elem)

    def copy(step):
        target = lax.rem(me + step, devices)
        return pltpu.make_async_remote_copy(
            src_ref=parts_ref.at[target],
            dst_ref=held.at[step],
            send_sem=send_sem.at[step],
            recv_sem=recv_sem.at[step],
            device_id=place(target),
            device_id_type=MESH,
        )

    @pl.loop(1, devices)
    def _(step):
        pl.semaphore_signal(
            barrier, inc=1, device_id=place(lax.rem(me + step, devices)), device_id_type=MESH
        )

    pl.semaphore_wait(barrier, devices - 1)

    @pl.loop(1, devices)
    def _(step):
        copy(step).start()

    held[0] = parts_ref[me]

    @pl.loop(1, devices)
    def _(step):
        copy(step).wait_recv()

    out_ref[0] = jnp.sum(held[...]) / columns

    @pl.loop(1, devices)
    def _(step):
        copy(step).wait_send()


def local(tables, state, speed_x, speed_y, w_in, b_in, w_mid, b_mid, w_top, b_top, w_out, b_out, span_of):
    feats, height, breadth = state.shape
    n_face, n_elem = lax.axis_size("face"), lax.axis_size("elem")
    devices = n_face * n_elem
    size = feats // CHUNKS
    steps = 3 * CHUNKS
    vmem = pl.BlockSpec(memory_space=pltpu.VMEM)
    hbm = pl.BlockSpec(memory_space=pl.ANY)
    n_out, hidden = w_out.shape

    final, inputs = pl.pallas_call(
        functools.partial(advect_kernel, n_face, n_elem, height, breadth),
        out_shape=(
            jax.ShapeDtypeStruct((feats * height, breadth), jnp.float32),
            jax.ShapeDtypeStruct((height // 2, feats, 2 * breadth), jnp.bfloat16),
        ),
        in_specs=[hbm, vmem, vmem, vmem, vmem],
        out_specs=(hbm, vmem),
        scratch_shapes=[
            pltpu.VMEM((feats * height, breadth), jnp.float32),
            pltpu.VMEM((height, feats, breadth), jnp.float32),
            pltpu.VMEM((height // NP * size, 8 * breadth), jnp.bfloat16),
            pltpu.VMEM((CHUNKS, 2, height // NP * size, 2 * breadth), jnp.float32),
            pltpu.VMEM((height // NP * size, NP * breadth), jnp.bfloat16),
            pltpu.VMEM((height // NP * size, NP * breadth), jnp.float32),
            pltpu.VMEM((steps, 2, size // 3, breadth), jnp.bfloat16),
            pltpu.VMEM((steps, 4, size // 3, breadth), jnp.bfloat16),
            pltpu.VMEM((steps, 2, size, breadth), jnp.bfloat16),
            pltpu.VMEM((steps, 2, size, breadth), jnp.bfloat16),
            pltpu.SemaphoreType.DMA((CHUNKS,)),
            pltpu.SemaphoreType.DMA((CHUNKS,)),
            pltpu.SemaphoreType.DMA((steps, 5)),
            pltpu.SemaphoreType.DMA((steps, 5)),
        ],
        compiler_params=pltpu.CompilerParams(
            collective_id=0, has_side_effects=True, vmem_limit_bytes=60 * 2**20
        ),
        name="advect",
    )(state.reshape(feats * height, breadth), jnp.stack([speed_x, speed_y], axis=1), *tables)

    bias = jnp.stack([b_in, b_mid, b_top, jnp.pad(b_out, (0, hidden - n_out))], axis=1)
    final, tend, parts = pl.pallas_call(
        functools.partial(physics_kernel, devices),
        out_shape=(
            jax.ShapeDtypeStruct((feats * height, breadth), jnp.float32),
            jax.ShapeDtypeStruct((n_out * height, breadth), jnp.bfloat16),
            jax.ShapeDtypeStruct((devices, 1, breadth), jnp.float32),
        ),
        in_specs=[hbm] + [vmem] * 7,
        out_specs=(hbm, vmem, vmem),
        scratch_shapes=[
            pltpu.VMEM((n_out * height, breadth), jnp.float32),
            pltpu.VMEM((height // 2, 2 * breadth), jnp.float32),
            pltpu.VMEM((height // 2, 2 * breadth), jnp.int32),
            pltpu.VMEM((feats * height, breadth), jnp.float32),
            pltpu.SemaphoreType.DMA((2,)),
        ],
        compiler_params=pltpu.CompilerParams(vmem_limit_bytes=60 * 2**20),
        name="physics",
    )(
        final,
        inputs,
        w_in,
        w_mid,
        w_top,
        w_out,
        bias,
        span_of.reshape(1, height * breadth),
    )
    span_heating = pl.pallas_call(
        functools.partial(totals_kernel, n_face, n_elem, height * breadth),
        out_shape=jax.ShapeDtypeStruct((1,), jnp.float32),
        in_specs=[vmem],
        out_specs=pl.BlockSpec(memory_space=pltpu.SMEM),
        scratch_shapes=[
            pltpu.VMEM((devices, 1, breadth), jnp.float32),
            pltpu.SemaphoreType.DMA((devices,)),
            pltpu.SemaphoreType.DMA((devices,)),
        ],
        compiler_params=pltpu.CompilerParams(collective_id=1, has_side_effects=True),
        name="totals",
    )(parts)
    return (
        final.reshape(state.shape),
        tend.reshape(n_out, height, breadth),
        span_heating,
    )


def solution(mesh):
    specs = (
        (P(None, "face", "elem"),) + (P(),) * 10 + (P("face", "elem", None, None),)
    )
    inner = jax.shard_map(
        local,
        mesh=mesh,
        in_specs=((P(), P(), P()),) + specs,
        out_specs=(P(None, "face", "elem"), P(None, "face", "elem"), P(("face", "elem"))),
        check_vma=False,
    )

    def whole(state, *rest):
        breadth = state.shape[2] // mesh.shape["elem"]
        made = (operator_tables(breadth),) + edge_tables(breadth)
        tables = tuple(jnp.asarray(table, dtype=jnp.bfloat16) for table in made)
        return inner(tables, state, *rest)

    return whole
```

```python
import functools
import math

import jax
import jax.numpy as jnp
import numpy as np
from jax import lax
from jax.experimental import pallas as pl
from jax.experimental.pallas import tpu as pltpu
from jax.sharding import PartitionSpec as P

NP = 4
LEV = 72
CHUNKS = 3
MESH = pl.DeviceIdType.MESH
SX_SLOT = (0, 1, 6, 7)
SY_SLOT = (2, 3, 4, 5)


def gll_matrix():
    inner_node = 1.0 / math.sqrt(5.0)
    nodes = np.array([-1.0, -inner_node, inner_node, 1.0])
    weights = np.array(
        [1.0 / np.prod([nodes[j] - nodes[k] for k in range(4) if k != j]) for j in range(4)]
    )
    matrix = np.zeros((4, 4))
    for i in range(4):
        for j in range(4):
            if i != j:
                matrix[i, j] = weights[j] / weights[i] / (nodes[i] - nodes[j])
    for i in range(4):
        matrix[i, i] = -np.sum(matrix[i])
    return matrix


def operator_tables(breadth):
    table = gll_matrix()
    deriv = np.kron(np.eye(breadth // NP), table)
    avg = np.eye(breadth)
    for j in range(breadth):
        if j % NP == NP - 1:
            avg[j, j] = 0.5
            if j + 1 < breadth:
                avg[j, j + 1] = 0.5
        elif j % NP == 0:
            avg[j, j] = 0.5
            if j > 0:
                avg[j, j - 1] = 0.5
    across = (avg @ deriv).T
    half = (0.5, 1.0, 1.0, 0.5)
    tables = []
    for pair, slots in enumerate(((0, 1, 2, 3, 4, 5), (2, 3, 4, 5, 6, 7))):
        out = np.zeros((6 * breadth, 2 * breadth))
        for col in range(2):
            j = 2 * pair + col
            for at, slot in enumerate(slots):
                if slot == SX_SLOT[j]:
                    block = half[j] * across
                elif slot in SY_SLOT:
                    block = half[j] * table[j, SY_SLOT.index(slot)] * avg.T
                else:
                    continue
                out[at * breadth : (at + 1) * breadth, col * breadth : (col + 1) * breadth] = block
        tables.append(out)
    return np.stack(tables).astype(np.float32)


def edge_tables(breadth):
    pick = np.zeros((NP * breadth, 2 * breadth), np.float32)
    place = np.zeros((breadth, NP * breadth), np.float32)
    for lane in range(breadth):
        j, side = divmod(lane % (2 * NP), 2)
        edge = 0 if side else breadth - 1
        pick[j * breadth + edge, lane] = 1.0
        pick[(NP - 1 - j) * breadth + edge, breadth + lane] = 1.0
        place[lane, j * breadth + (breadth - 1 if side else 0)] = 1.0
    return pick, place


def to_columns(sources, lines, columns):
    lines[...] = jnp.zeros_like(lines)
    for at, source in enumerate(sources):
        lines[at : at + 1, 0 : source.shape[1]] = source[...]
    columns[...] = lines[...].T


def advect_kernel(
    n_face,
    n_elem,
    height,
    breadth,
    state_hbm,
    speed_x,
    speed_y,
    table_ref,
    pick_ref,
    place_ref,
    final_hbm,
    inputs_ref,
    field,
    base,
    slots,
    raw,
    rows16,
    edged,
    lines,
    speed_ref,
    x_send,
    x_recv,
    y_send,
    y_recv,
    load_sem,
    store_sem,
    send_sem,
    recv_sem,
):
    feats = speed_x.shape[1]
    size = feats // CHUNKS
    rows = size * height
    elements = height // NP
    face, elem = lax.axis_index("face"), lax.axis_index("elem")
    other = lax.rem(face + 1, n_face)
    right, left = lax.rem(elem + 1, n_elem), lax.rem(elem + n_elem - 1, n_elem)
    partners = ((face, left), (face, right), (other, left), (other, right), (other, elem))

    def load(chunk):
        at = pl.ds(chunk * rows, rows)
        return pltpu.make_async_copy(state_hbm.at[at], field.at[at], load_sem.at[chunk])

    def store(chunk):
        at = pl.ds(chunk * rows, rows)
        return pltpu.make_async_copy(field.at[at], final_hbm.at[at], store_sem.at[chunk])

    for chunk in range(CHUNKS):
        load(chunk).start()

    to_columns((speed_x, speed_y), lines, speed_ref)
    barrier = pltpu.get_barrier_semaphore()
    for partner in partners:
        pl.semaphore_signal(barrier, inc=1, device_id=partner, device_id_type=MESH)
    pl.semaphore_wait(barrier, len(partners))

    def copies(step):
        made = []
        for at in range(4):
            made.append(
                pltpu.make_async_remote_copy(
                    src_ref=x_send.at[step, at // 2],
                    dst_ref=x_recv.at[step, at],
                    send_sem=send_sem.at[step, at],
                    recv_sem=recv_sem.at[step, at],
                    device_id=partners[at],
                    device_id_type=MESH,
                )
            )
        made.append(
            pltpu.make_async_remote_copy(
                src_ref=y_send.at[step],
                dst_ref=y_recv.at[step],
                send_sem=send_sem.at[step, 4],
                recv_sem=recv_sem.at[step, 4],
                device_id=partners[4],
                device_id_type=MESH,
            )
        )
        return made

    lane = lax.broadcasted_iota(jnp.int32, (16, breadth), 1)
    groups = 3
    trips = size // (16 * groups)

    def speeds(chunk, at):
        pair = speed_ref[pl.ds(pl.multiple_of(chunk * size + at, 16), 16), :]
        across = jnp.broadcast_to(-pair[:, 0:1], (16, breadth))
        down = jnp.broadcast_to(-pair[:, 1:2], (16, breadth))
        return across, down

    def put_slots(at, y, value, across, down):
        element, j = divmod(y, NP)
        place = pl.ds(pl.multiple_of(element * size + at, 16), 16)
        sx, sy = SX_SLOT[j] * breadth, SY_SLOT[j] * breadth
        slots[place, sx : sx + breadth] = (across * value).astype(jnp.bfloat16)
        slots[place, sy : sy + breadth] = (down * value).astype(jnp.bfloat16)

    def field_at(chunk, at, y):
        return pl.ds((chunk * size + at) * height + y, 16, stride=height)

    def raw_at(chunk, at, y):
        element, j = divmod(y, NP)
        place = pl.ds(pl.multiple_of(element * size + at, 16), 16)
        return raw[chunk, j // 2, place, (j % 2) * breadth : (j % 2 + 1) * breadth]

    def prepare(chunk):
        @pl.loop(0, size // 16)
        def _(block):
            at = block * 16
            across, down = speeds(chunk, at)
            for y in range(height):
                put_slots(at, y, field[field_at(chunk, at, y), :], across, down)

    def apply_and_send(stage, chunk):
        step = stage * CHUNKS + chunk
        for pair in range(2):
            raw[chunk, pair] = jnp.dot(
                slots[:, 2 * pair * breadth : (2 * pair + 6) * breadth],
                table_ref[pair],
                preferred_element_type=jnp.float32,
            )
        y_send[step, 0] = raw[chunk, 0, 0:size, 0:breadth].astype(jnp.bfloat16)
        y_send[step, 1] = raw[
            chunk, 1, (elements - 1) * size : elements * size, breadth : 2 * breadth
        ].astype(jnp.bfloat16)

        for pair in range(2):
            rows16[:, 2 * pair * breadth : 2 * (pair + 1) * breadth] = raw[chunk, pair].astype(
                jnp.bfloat16
            )
        edged[:, 0 : 2 * breadth] = jnp.dot(
            rows16[...], pick_ref[...], preferred_element_type=jnp.float32
        )

        @pl.loop(0, trips)
        def _(trip):
            for kind in range(2):
                packed = jnp.zeros((16, breadth), jnp.float32)
                for group in range(groups):
                    at = (trip * groups + group) * 16
                    for element in range(elements):
                        there = edged[
                            pl.ds(pl.multiple_of(element * size + at, 16), 16),
                            kind * breadth : (kind + 1) * breadth,
                        ]
                        spot = elements - 1 - element if kind else element
                        packed = jnp.where(
                            lane // (2 * NP) == elements * group + spot, there, packed
                        )
                x_send[step, kind, pl.ds(pl.multiple_of(trip * 16, 16), 16), :] = packed.astype(
                    jnp.bfloat16
                )

        for copy in copies(step):
            copy.start()

    def finish(stage, chunk):
        step = stage * CHUNKS + chunk
        for copy in copies(step):
            copy.wait_recv()

        @pl.loop(0, trips)
        def _(trip):
            packed_at = pl.ds(pl.multiple_of(trip * 16, 16), 16)

            def merged(first):
                from_right = x_recv[step, first, packed_at, :].astype(jnp.float32)
                from_left = x_recv[step, first + 1, packed_at, :].astype(jnp.float32)
                return jnp.where(lane % 2 == 0, from_left, from_right)

            y_of = lane // 2 % height
            outer = (y_of == 0) | (y_of == height - 1)
            total = merged(0) + jnp.where(outer, merged(2), 0.0)
            for group in range(groups):
                at = (trip * groups + group) * 16
                for element in range(elements):
                    own_lanes = lane // (2 * NP) == elements * group + element
                    rows16[pl.ds(pl.multiple_of(element * size + at, 16), 16), 0:breadth] = (
                        jnp.where(own_lanes, total, 0.0).astype(jnp.bfloat16)
                    )

        edged[...] = jnp.dot(
            rows16[:, 0:breadth], place_ref[...], preferred_element_type=jnp.float32
        )

        @pl.loop(0, trips)
        def _(trip):
            for group in range(groups):
                at = (trip * groups + group) * 16

                def own(y):
                    element, j = divmod(y, NP)
                    added = edged[
                        pl.ds(pl.multiple_of(element * size + at, 16), 16),
                        j * breadth : (j + 1) * breadth,
                    ]
                    return raw_at(chunk, at, y) + added

                def across_face(row):
                    there = y_recv[step, row, pl.ds(pl.multiple_of(at, 16), 16), :]
                    return there.astype(jnp.float32)

                across, down = speeds(chunk, at)

                def update(y, tendency):
                    kept = pl.ds(pl.multiple_of(chunk * size + at, 16), 16)
                    if stage == 0:
                        first = field[field_at(chunk, at, y), :]
                        base[y, kept, :] = first + 0.25 * tendency
                        value = first + tendency
                    elif stage == 1:
                        first = field[field_at(chunk, at, y), :]
                        value = base[y, kept, :] + 0.25 * tendency
                        base[y, kept, :] = first * (1.0 / 3.0) + value * (2.0 / 3.0)
                    else:
                        value = base[y, kept, :] + (2.0 / 3.0) * tendency
                        field[field_at(chunk, at, y), :] = value
                        half = (y % 2) * breadth
                        inputs_ref[y // 2, kept, half : half + breadth] = value.astype(
                            jnp.bfloat16
                        )
                        return
                    put_slots(at, y, value, across, down)

                for y in range(height):
                    if y == 0:
                        update(y, own(y) + across_face(1))
                    elif y == height - 1:
                        update(y, own(y) + across_face(0))
                    elif y % NP == NP - 1:
                        both = own(y) + own(y + 1)
                        update(y, both)
                        update(y + 1, both)
                    elif y % NP != 0:
                        update(y, own(y))

    @pl.loop(0, CHUNKS)
    def _(chunk):
        load(chunk).wait()
        prepare(chunk)
        apply_and_send(0, chunk)

    for stage in (1, 2):

        @pl.loop(0, CHUNKS)
        def _(chunk):
            finish(stage - 1, chunk)
            apply_and_send(stage, chunk)

    @pl.loop(0, CHUNKS)
    def _(chunk):
        finish(2, chunk)
        store(chunk).start()

    @pl.loop(0, 3 * CHUNKS)
    def _(step):
        for copy in copies(step):
            copy.wait_send()

    for chunk in range(CHUNKS):
        store(chunk).wait()


def physics_kernel(
    devices,
    final_hbm,
    inputs_ref,
    w_in,
    w_mid,
    w_top,
    w_out,
    b_in,
    b_mid,
    b_top,
    b_out,
    span_ref,
    copied_hbm,
    tend_ref,
    parts_ref,
    outs,
    heat,
    spans,
    staged,
    lines,
    bias_ref,
    copy_sem,
):
    pairs, _, width = inputs_ref.shape
    breadth = width // 2
    height = 2 * pairs
    n_out = w_out.shape[0]
    fetch = pltpu.make_async_copy(final_hbm, staged, copy_sem.at[0])
    write = pltpu.make_async_copy(staged, copied_hbm, copy_sem.at[1])
    fetch.start()
    to_columns((b_in, b_mid, b_top, b_out), lines, bias_ref)
    for pair in range(pairs):
        spans[pair : pair + 1, :] = span_ref[:, pair * width : (pair + 1) * width]

    def silu(value):
        half = 0.5 * value
        return (half + half * jnp.tanh(half)).astype(jnp.bfloat16)

    def columns(pair):
        hidden = inputs_ref[pair]
        for layer, weight in enumerate((w_in, w_mid, w_top)):
            hidden = silu(
                jnp.dot(weight[...], hidden, preferred_element_type=jnp.float32)
                + bias_ref[:, layer : layer + 1]
            )
        out = (
            jnp.dot(w_out[...], hidden, preferred_element_type=jnp.float32)
            + bias_ref[0:n_out, 3:4]
        )
        heat[pl.ds(pair, 1), :] = jnp.sum(out[:LEV], axis=0, keepdims=True)
        for side in range(2):
            outs[pl.ds(2 * pair + side, n_out, stride=height), :] = out[
                :, side * breadth : (side + 1) * breadth
            ]

    pl.loop(0, pairs // 2)(columns)
    fetch.wait()
    write.start()
    pl.loop(pairs // 2, pairs)(columns)

    step = 15 * height

    @pl.loop(0, n_out * height // step)
    def _(block):
        at = pl.ds(pl.multiple_of(block * step, step), step)
        tend_ref[at, :] = outs[at, :].astype(jnp.bfloat16)

    @pl.loop(0, devices)
    def _(span):
        part = jnp.where(spans[...] == span, heat[...], 0.0)
        line = jnp.sum(part, axis=0, keepdims=True)
        parts_ref[span] = line[:, :breadth] + line[:, breadth:]

    write.wait()


def totals_kernel(n_face, n_elem, columns, parts_ref, out_ref, held, send_sem, recv_sem):
    devices = n_face * n_elem
    me = lax.axis_index("face") * n_elem + lax.axis_index("elem")
    barrier = pltpu.get_barrier_semaphore()

    def place(number):
        return (number // n_elem, number % n_elem)

    def copy(step):
        target = lax.rem(me + step, devices)
        return pltpu.make_async_remote_copy(
            src_ref=parts_ref.at[target],
            dst_ref=held.at[step],
            send_sem=send_sem.at[step],
            recv_sem=recv_sem.at[step],
            device_id=place(target),
            device_id_type=MESH,
        )

    @pl.loop(1, devices)
    def _(step):
        pl.semaphore_signal(
            barrier, inc=1, device_id=place(lax.rem(me + step, devices)), device_id_type=MESH
        )

    pl.semaphore_wait(barrier, devices - 1)

    @pl.loop(1, devices)
    def _(step):
        copy(step).start()

    held[0] = parts_ref[me]

    @pl.loop(1, devices)
    def _(step):
        copy(step).wait_recv()

    out_ref[0] = jnp.sum(held[...]) / columns

    @pl.loop(1, devices)
    def _(step):
        copy(step).wait_send()


def local(tables, state, speed_x, speed_y, w_in, b_in, w_mid, b_mid, w_top, b_top, w_out, b_out, span_of):
    feats, height, breadth = state.shape
    n_face, n_elem = lax.axis_size("face"), lax.axis_size("elem")
    devices = n_face * n_elem
    size = feats // CHUNKS
    steps = 3 * CHUNKS
    vmem = pl.BlockSpec(memory_space=pltpu.VMEM)
    hbm = pl.BlockSpec(memory_space=pl.ANY)
    n_out, hidden = w_out.shape

    final, inputs = pl.pallas_call(
        functools.partial(advect_kernel, n_face, n_elem, height, breadth),
        out_shape=(
            jax.ShapeDtypeStruct((feats * height, breadth), jnp.float32),
            jax.ShapeDtypeStruct((height // 2, feats, 2 * breadth), jnp.bfloat16),
        ),
        in_specs=[hbm] + [vmem] * 5,
        out_specs=(hbm, vmem),
        scratch_shapes=[
            pltpu.VMEM((feats * height, breadth), jnp.float32),
            pltpu.VMEM((height, feats, breadth), jnp.float32),
            pltpu.VMEM((height // NP * size, 8 * breadth), jnp.bfloat16),
            pltpu.VMEM((CHUNKS, 2, height // NP * size, 2 * breadth), jnp.float32),
            pltpu.VMEM((height // NP * size, NP * breadth), jnp.bfloat16),
            pltpu.VMEM((height // NP * size, NP * breadth), jnp.float32),
            pltpu.VMEM((8, hidden), jnp.float32),
            pltpu.VMEM((hidden, 8), jnp.float32),
            pltpu.VMEM((steps, 2, size // 3, breadth), jnp.bfloat16),
            pltpu.VMEM((steps, 4, size // 3, breadth), jnp.bfloat16),
            pltpu.VMEM((steps, 2, size, breadth), jnp.bfloat16),
            pltpu.VMEM((steps, 2, size, breadth), jnp.bfloat16),
            pltpu.SemaphoreType.DMA((CHUNKS,)),
            pltpu.SemaphoreType.DMA((CHUNKS,)),
            pltpu.SemaphoreType.DMA((steps, 5)),
            pltpu.SemaphoreType.DMA((steps, 5)),
        ],
        compiler_params=pltpu.CompilerParams(
            collective_id=0, has_side_effects=True, vmem_limit_bytes=60 * 2**20
        ),
        name="advect",
    )(state.reshape(feats * height, breadth), speed_x[None], speed_y[None], *tables)

    final, tend, parts = pl.pallas_call(
        functools.partial(physics_kernel, devices),
        out_shape=(
            jax.ShapeDtypeStruct((feats * height, breadth), jnp.float32),
            jax.ShapeDtypeStruct((n_out * height, breadth), jnp.bfloat16),
            jax.ShapeDtypeStruct((devices, 1, breadth), jnp.float32),
        ),
        in_specs=[hbm] + [vmem] * 10,
        out_specs=(hbm, vmem, vmem),
        scratch_shapes=[
            pltpu.VMEM((n_out * height, breadth), jnp.float32),
            pltpu.VMEM((height // 2, 2 * breadth), jnp.float32),
            pltpu.VMEM((height // 2, 2 * breadth), jnp.int32),
            pltpu.VMEM((feats * height, breadth), jnp.float32),
            pltpu.VMEM((8, hidden), jnp.float32),
            pltpu.VMEM((hidden, 8), jnp.float32),
            pltpu.SemaphoreType.DMA((2,)),
        ],
        compiler_params=pltpu.CompilerParams(vmem_limit_bytes=60 * 2**20),
        name="physics",
    )(
        final,
        inputs,
        w_in,
        w_mid,
        w_top,
        w_out,
        b_in[None],
        b_mid[None],
        b_top[None],
        b_out[None],
        span_of.reshape(1, height * breadth),
    )
    span_heating = pl.pallas_call(
        functools.partial(totals_kernel, n_face, n_elem, height * breadth),
        out_shape=jax.ShapeDtypeStruct((1,), jnp.float32),
        in_specs=[vmem],
        out_specs=pl.BlockSpec(memory_space=pltpu.SMEM),
        scratch_shapes=[
            pltpu.VMEM((devices, 1, breadth), jnp.float32),
            pltpu.SemaphoreType.DMA((devices,)),
            pltpu.SemaphoreType.DMA((devices,)),
        ],
        compiler_params=pltpu.CompilerParams(collective_id=1, has_side_effects=True),
        name="totals",
    )(parts)
    return (
        final.reshape(state.shape),
        tend.reshape(n_out, height, breadth),
        span_heating,
    )


def solution(mesh):
    specs = (
        (P(None, "face", "elem"),) + (P(),) * 10 + (P("face", "elem", None, None),)
    )
    inner = jax.shard_map(
        local,
        mesh=mesh,
        in_specs=((P(), P(), P()),) + specs,
        out_specs=(P(None, "face", "elem"), P(None, "face", "elem"), P(("face", "elem"))),
        check_vma=False,
    )

    def whole(state, *rest):
        breadth = state.shape[2] // mesh.shape["elem"]
        made = (operator_tables(breadth),) + edge_tables(breadth)
        tables = tuple(jnp.asarray(table, dtype=jnp.bfloat16) for table in made)
        return inner(tables, state, *rest)

    return whole
```
